32 devices in a mesh: dp: 16 (over z, x, core), seq: 2 (over y).
Axes of the slice: x: 2, y: 2, z: 4, core: 2. Of those that a mesh axis runs over, the one named last changes fastest.
Arguments:
- queries: bfloat16 [16, 768, 1536], P('dp', 'seq'), may hold values from -16 to 16
- key_rows: bfloat16 [16, 768, 1536], P('dp', 'seq'), may hold values from -16 to 16
- value_rows: bfloat16 [16, 768, 1536], P('dp', 'seq'), may hold values from -6 to 6
- out_grad: bfloat16 [16, 768, 1536], P('dp', 'seq'), may hold values from -6 to 6
- w_out: bfloat16 [1536, 1536], P('dp'), may hold values from -0.15625 to 0.15625
- band_start: int32 [16], P('dp'), may hold values from 0 to 1
- window_active: int32 [2, 3], replicated, may hold values from 0 to 1
Outputs:
- query_grad: bfloat16 [16, 768, 1536], P('dp', 'seq')
- key_grad: bfloat16 [16, 768, 1536], P('dp', 'seq')
- value_grad: bfloat16 [16, 768, 1536], P('dp', 'seq')
- weight_grad: float32 [1536, 1536], P('dp')
The draws below stay inside these ranges and needn't reach their ends.
All inputs are finite; a program needn't handle non-finite values.
Results may differ from the reference program's by a relative error of at most 0.011.
Values may be sent and summed in bfloat16 or wider, within the bound.
A program may use at most 128 MiB of HBM per device.

```python
import math
from functools import partial
import jax
import jax.numpy as jnp
from jax import lax

HEADS = 12
HS = 128
DW = 1536
TILE = 384
HD = 1536
NT = 2
BAND = 768
CLIPS = 16


def base_rows(key, part, fold_value):
    mixed_key = jax.random.fold_in(jax.random.fold_in(key, fold_value), part)
    base_key, scale_key = jax.random.split(mixed_key)
    full_shape = (CLIPS, NT, TILE, HEADS, HS)
    base_draw = jnp.clip(jax.random.normal(base_key, full_shape, jnp.float32), -4.5, 4.5)
    row_scale = jnp.exp(jax.random.uniform(scale_key, (CLIPS, NT, TILE, HEADS, 1), jnp.float32, math.log(0.35), 0.0))
    return base_draw * row_scale


def draw_queries(key, part):
    values_out = base_rows(key, part, 2)
    return values_out.reshape(CLIPS, NT * TILE, HEADS * HS).astype(jnp.bfloat16)


def draw_key_rows(key, part):
    values_out = base_rows(key, part, 3)
    return values_out.reshape(CLIPS, NT * TILE, HEADS * HS).astype(jnp.bfloat16)


def draw_band_start(key, part):
    mixed_key = jax.random.fold_in(jax.random.fold_in(key, 11), part)
    value_key, order_key = jax.random.split(mixed_key)
    starts = jax.random.randint(value_key, (CLIPS,), 0, NT).astype(jnp.int32)
    order = jax.random.permutation(order_key, CLIPS)
    slots = jnp.arange(CLIPS, dtype=jnp.int32)
    starts = jnp.where(slots == order[0], 0, starts)
    starts = jnp.where(slots == order[1], NT - 1, starts)
    return starts.astype(jnp.int32)


def draw_window_active(key, part):
    mixed_key = jax.random.fold_in(jax.random.fold_in(key, 13), part)
    value_key, order_key = jax.random.split(mixed_key)
    flags = jax.random.randint(value_key, (NT * 3,), 0, 2).astype(jnp.int32)
    order = jax.random.permutation(order_key, NT * 3)
    slots = jnp.arange(NT * 3, dtype=jnp.int32)
    flags = jnp.where(slots == order[0], 0, flags)
    flags = jnp.where(slots == order[1], 1, flags)
    return flags.reshape(NT, 3).astype(jnp.int32)


def block_scale(own_key, extent, cuts, least, largest):
    def one(position, shards_of):
        steps = jax.random.uniform(jax.random.fold_in(jax.random.fold_in(own_key, 6), position), (shards_of,), jnp.float32, least / len(cuts), largest / len(cuts))
        return jnp.repeat(jnp.exp(steps), extent[position] // shards_of).reshape((-1,) + (1,) * (len(extent) - position - 1))

    factor_of = one(*cuts[0])
    for cut in cuts[1:]:
        factor_of = factor_of * one(*cut)
    return factor_of


def bell_draw(rng, extent, scale, limit, cuts=(), kind=jnp.bfloat16):
    factor_of = block_scale(rng, extent, cuts, -0.22, 0.18) if cuts else 1.0
    result = jax.random.normal(rng, extent, jnp.float32) * scale * factor_of
    return jnp.minimum(jnp.maximum(result, -limit), limit).astype(kind)


def setup_inputs(seed: int = 0) -> dict:
    seeds = jax.random.split(jax.random.key(seed), 8)
    queries = draw_queries(jax.random.fold_in(seeds[7], 71), 0)
    key_rows = draw_key_rows(jax.random.fold_in(seeds[7], 71), 0)
    value_rows = bell_draw(seeds[2], (CLIPS, BAND, HD), 1.0, 6.0, ((0, 16), (1, 2)))
    out_grad = bell_draw(seeds[3], (CLIPS, BAND, DW), 1.0, 6.0, ((0, 16), (1, 2)))
    w_out = bell_draw(seeds[4], (HD, DW), HD ** -0.5, 0.15625, ((0, 16),))
    band_start = draw_band_start(jax.random.fold_in(seeds[7], 71), 0)
    window_active = draw_window_active(jax.random.fold_in(seeds[7], 71), 0)
    return dict(queries=queries, key_rows=key_rows, value_rows=value_rows, out_grad=out_grad, w_out=w_out, band_start=band_start, window_active=window_active)


def window_mask(window_active, tile_index):
    table_ids = jnp.arange(window_active.shape[0], dtype=jnp.int32)
    picked = (table_ids[None, :] == tile_index[:, None]).astype(jnp.int32)
    flags = lax.optimization_barrier(jnp.sum(picked[:, :, None] * window_active[None, :, :], axis=1))
    centre = (jnp.arange(3, dtype=jnp.int32) == 1)[None, :]
    return (flags == 1) | centre

def bf16_round(values_in):
    return lax.optimization_barrier(values_in.astype(jnp.bfloat16)).astype(jnp.float32)

def block_grads(operands):
    query_block, key_band, value_band, key_bias, grad_block = operands
    score_scale = HS ** (-0.5)
    query_heads = query_block.astype(jnp.float32).reshape(TILE, HEADS, HS)
    key_heads = key_band.astype(jnp.float32).reshape(3 * TILE, HEADS, HS)
    value_heads = value_band.astype(jnp.float32).reshape(3 * TILE, HEADS, HS)
    grad_heads = grad_block.astype(jnp.float32).reshape(TILE, HEADS, HS)
    scores = jnp.einsum('qhd,khd->hqk', query_heads, key_heads) * score_scale + key_bias[None, None, :]
    row_max = lax.optimization_barrier(jnp.max(scores, axis=2, keepdims=True))
    exp_scores = jnp.exp(scores - row_max)
    row_sum = lax.optimization_barrier(jnp.sum(exp_scores, axis=2, keepdims=True))
    weights = bf16_round(exp_scores / row_sum)
    attended = jnp.einsum('hqk,khd->qhd', weights, value_heads).astype(jnp.bfloat16)
    log_total = row_max + jnp.log(row_sum)
    prob_full = jnp.exp(scores - log_total)
    row_delta = jnp.einsum('qhd,qhd->hq', grad_heads, attended.astype(jnp.float32))
    prob_weights = bf16_round(prob_full)
    value_part = jnp.einsum('hqk,qhd->khd', prob_weights, grad_heads)
    prob_grad = jnp.einsum('qhd,khd->hqk', grad_heads, value_heads)
    score_grad = bf16_round(prob_full * (prob_grad - row_delta[:, :, None]))
    query_part = jnp.einsum('hqk,khd->qhd', score_grad, key_heads) * score_scale
    key_part = jnp.einsum('hqk,qhd->khd', score_grad, query_heads) * score_scale
    return (attended.reshape(TILE, HEADS * HS), query_part.reshape(TILE, HEADS * HS).astype(jnp.bfloat16), key_part.reshape(3 * TILE, HEADS * HS), value_part.reshape(3 * TILE, HEADS * HS))

def clip_grads(w_out, window_active, weight_acc, operands):
    clip_queries, clip_keys, clip_values, clip_grad, clip_start = operands
    feat_width = HEADS * HS
    attended_grad = jnp.dot(clip_grad, w_out.T, preferred_element_type=jnp.float32).astype(jnp.bfloat16)
    tile_index = jnp.mod(jnp.arange(NT, dtype=jnp.int32) - clip_start, NT).astype(jnp.int32)
    active = window_mask(window_active, tile_index)
    key_bias = jnp.repeat(jnp.where(active, 0.0, -jnp.inf).astype(jnp.float32), TILE, axis=1)
    key_blocks = clip_keys.reshape(NT, TILE, feat_width)
    value_blocks = clip_values.reshape(NT, TILE, feat_width)
    key_band = jnp.concatenate((jnp.roll(key_blocks, 1, axis=0), key_blocks, jnp.roll(key_blocks, -1, axis=0)), axis=1)
    value_band = jnp.concatenate((jnp.roll(value_blocks, 1, axis=0), value_blocks, jnp.roll(value_blocks, -1, axis=0)), axis=1)
    attended, query_grad, key_parts, value_parts = lax.map(block_grads, (clip_queries.reshape(NT, TILE, feat_width), key_band, value_band, key_bias, attended_grad.reshape(NT, TILE, feat_width)))
    key_parts = key_parts.reshape(NT, 3, TILE, feat_width)
    value_parts = value_parts.reshape(NT, 3, TILE, feat_width)
    key_grad = key_parts[:, 1] + jnp.roll(key_parts[:, 0], -1, axis=0) + jnp.roll(key_parts[:, 2], 1, axis=0)
    value_grad = value_parts[:, 1] + jnp.roll(value_parts[:, 0], -1, axis=0) + jnp.roll(value_parts[:, 2], 1, axis=0)
    weight_acc = weight_acc + jnp.dot(attended.reshape(BAND, feat_width).T, clip_grad, preferred_element_type=jnp.float32)
    return (weight_acc, (query_grad.reshape(BAND, feat_width), key_grad.astype(jnp.bfloat16).reshape(BAND, feat_width), value_grad.astype(jnp.bfloat16).reshape(BAND, feat_width)))

def reference(queries, key_rows, value_rows, out_grad, w_out, band_start, window_active):
    start_acc = jnp.zeros((HEADS * HS, DW), jnp.float32)
    weight_acc, grads = lax.scan(partial(clip_grads, w_out, window_active), start_acc, (queries, key_rows, value_rows, out_grad, band_start))
    weight_grad = weight_acc / math.sqrt(CLIPS * BAND)
    return (grads[0], grads[1], grads[2], weight_grad)
```

```python
import functools
import math

import jax
import jax.numpy as jnp
from jax import lax
from jax.experimental import pallas as pl
from jax.experimental.pallas import tpu as pltpu
from jax.sharding import PartitionSpec as P

HEADS = 12
HS = 128
CHUNKS = (4, 4, 4)
SCALE = HS ** (-0.5)
LOG2E = 1.4426950408889634
VMEM_LIMIT = 48 * 1024 * 1024

NT_DIMS = (((1,), (1,)), ((), ()))
TN_DIMS = (((0,), (0,)), ((), ()))
NN_DIMS = (((1,), (0,)), ((), ()))


def mm(lhs, rhs, dims):
    return lax.dot_general(lhs, rhs, dims, preferred_element_type=jnp.float32)


def passed_along(value, axis, steps):
    count = lax.axis_size(axis)
    pairs = [(source, (source + steps) % count) for source in range(count)]
    return lax.ppermute(value, axis, pairs)


def forward_kernel(other_count, bias_ref, q_ref, k_ref, v_ref, *refs):
    other_refs = refs[:other_count]
    att_ref, lse_ref = refs[-2:]
    query = q_ref[...]
    scores = [mm(k_ref[...], query, NT_DIMS) * (SCALE * LOG2E)]
    values = [v_ref[...]]
    for place, other_ref in enumerate(other_refs):
        scores.append(mm(other_ref[0], query, NT_DIMS) * (SCALE * LOG2E) + bias_ref[place])
        values.append(other_ref[1])
    row_max = functools.reduce(
        jnp.maximum, [jnp.max(block, axis=0, keepdims=True) for block in scores]
    )
    total = 0.0
    mixed = 0.0
    for block, value in zip(scores, values):
        weights = jnp.exp2(block - row_max)
        total = total + jnp.sum(weights, axis=0, keepdims=True)
        mixed = mixed + mm(value, weights.astype(jnp.bfloat16), TN_DIMS)
    att_ref[...] = jnp.transpose(mixed / total).astype(att_ref.dtype)
    lse_ref[0] = jnp.broadcast_to(row_max + jnp.log2(total), lse_ref.shape[1:])


def backward_kernel(
    other_count, bias_ref, q_ref, k_ref, v_ref, att_ref, lse_ref, og_ref, w_ref, *refs
):
    other_refs = refs[:other_count]
    dq_ref, own_ref = refs[-2 - other_count : len(refs) - other_count]
    out_refs = refs[len(refs) - other_count :]
    query = q_ref[...]
    grad = mm(og_ref[...], w_ref[...], NT_DIMS).astype(jnp.bfloat16)
    product = grad.astype(jnp.float32) * att_ref[...].astype(jnp.float32)
    delta = jnp.sum(jnp.transpose(product), axis=0, keepdims=True)
    log_total = lse_ref[0][0:1]
    query_part = 0.0
    for place in range(other_count + 1):
        if place == 0:
            key, value, shift = k_ref[...], v_ref[...], log_total
        else:
            key, value = other_refs[place - 1][0], other_refs[place - 1][1]
            shift = log_total - bias_ref[place - 1]
        prob = jnp.exp2(mm(key, query, NT_DIMS) * (SCALE * LOG2E) - shift)
        value_part = mm(prob.astype(jnp.bfloat16), grad, NN_DIMS)
        score_grad = (prob * (mm(value, grad, NT_DIMS) - delta)).astype(jnp.bfloat16)
        key_part = mm(score_grad, query, NN_DIMS) * SCALE
        query_part = query_part + mm(key, score_grad, TN_DIMS)
        target = own_ref if place == 0 else out_refs[place - 1]
        target[0] = key_part.astype(target.dtype)
        target[1] = value_part.astype(target.dtype)
    dq_ref[...] = jnp.transpose(query_part * SCALE).astype(dq_ref.dtype)


def add_kernel(other_count, own_ref, *refs):
    dk_ref, dv_ref = refs[-2:]
    keys, values = own_ref[0], own_ref[1]
    for ref in refs[:other_count]:
        keys = keys + ref[0].astype(jnp.float32)
        values = values + ref[1].astype(jnp.float32)
    dk_ref[...] = keys.astype(dk_ref.dtype)
    dv_ref[...] = values.astype(dv_ref.dtype)


def params():
    return pltpu.CompilerParams(vmem_limit_bytes=VMEM_LIMIT)


def cost(flops, moved, exps):
    return pl.CostEstimate(flops=int(flops), bytes_accessed=int(moved), transcendentals=int(exps))


def column_block(rows, first):
    return pl.BlockSpec((rows, HS), lambda i: (0, first + i))


def pair_block(rows):
    return pl.BlockSpec((2, rows, HS), lambda i: (0, 0, i))


SMEM_BLOCK = pl.BlockSpec(memory_space=pltpu.SMEM)
HBM_BLOCK = pl.BlockSpec(memory_space=pl.ANY)


def forward(first, heads, bias, q, k, v, others, att):
    rows, width = q.shape
    count = len(others)
    head = column_block(rows, first)
    chained = [] if att is None else [att]
    return pl.pallas_call(
        functools.partial(forward_kernel, count),
        grid=(heads,),
        in_specs=[SMEM_BLOCK, head, head, head]
        + [pair_block(rows)] * count
        + [HBM_BLOCK] * len(chained),
        out_specs=[head, pl.BlockSpec((1, 8, rows), lambda i: (i, 0, 0))],
        out_shape=[
            jax.ShapeDtypeStruct((rows, width), jnp.bfloat16),
            jax.ShapeDtypeStruct((heads, 8, rows), jnp.float32),
        ],
        input_output_aliases={4 + count: 0} if chained else {},
        compiler_params=params(),
        cost_estimate=cost(
            heads * (count + 1) * rows * rows * HS * 4,
            heads * rows * HS * 2 * (4 + 2 * count),
            heads * (count + 1) * rows * rows,
        ),
        name="attend",
    )(bias, q, k, v, *others, *chained)


def backward(first, heads, bias, q, k, v, att, lse, og, w, others, dq):
    rows, width = q.shape
    count = len(others)
    head = column_block(rows, first)
    chained = [] if dq is None else [dq]
    results = pl.pallas_call(
        functools.partial(backward_kernel, count),
        grid=(heads,),
        in_specs=[SMEM_BLOCK, head, head, head, head]
        + [
            pl.BlockSpec((1, 8, rows), lambda i: (i, 0, 0)),
            pl.BlockSpec(og.shape, lambda i: (0, 0)),
            pl.BlockSpec((HS, w.shape[1]), lambda i: (first + i, 0)),
        ]
        + [pair_block(rows)] * count
        + [HBM_BLOCK] * len(chained),
        out_specs=[head] + [pair_block(rows)] * (count + 1),
        out_shape=[
            jax.ShapeDtypeStruct((rows, width), jnp.bfloat16),
            jax.ShapeDtypeStruct((2, rows, heads * HS), jnp.float32),
        ]
        + [jax.ShapeDtypeStruct((2, rows, heads * HS), jnp.bfloat16)] * count,
        input_output_aliases={8 + count: 0} if chained else {},
        compiler_params=params(),
        cost_estimate=cost(
            heads * ((count + 1) * rows * rows * HS * 10 + rows * HS * width * 2),
            heads * rows * HS * 2 * (8 + 8 * count),
            heads * (count + 1) * rows * rows,
        ),
        name="attend_grad",
    )(bias, q, k, v, att, lse, og, w, *others, *chained)
    return results[0], results[1], results[2:]


def add_parts(first, heads, rows, width, own, received, chained):
    count = len(received)
    head = column_block(rows, first)
    return pl.pallas_call(
        functools.partial(add_kernel, count),
        grid=(heads,),
        in_specs=[pair_block(rows)] * (count + 1) + [HBM_BLOCK] * len(chained),
        out_specs=[head, head],
        out_shape=[jax.ShapeDtypeStruct((rows, width), jnp.bfloat16)] * 2,
        input_output_aliases={1 + count: 0, 2 + count: 1} if chained else {},
        compiler_params=params(),
        cost_estimate=cost(0, heads * rows * HS * 2 * (6 + 2 * count), 0),
        name="add_parts",
    )(own, *received, *chained)


def exchange_bit(value, bit):
    count = lax.axis_size("dp")
    return lax.ppermute(value, "dp", [(source, source ^ (1 << bit)) for source in range(count)])


def summed_rows(att, og, norm):
    place = lax.axis_index("dp")
    bits = lax.axis_size("dp").bit_length() - 1
    rows, width = att.shape
    block = width >> bits
    core = lax.rem(place, 2)
    panels = att.reshape(rows, width // (2 * block), 2, block)

    def side(which):
        return lax.dynamic_index_in_dim(panels, which, 2, keepdims=False).reshape(rows, width // 2)

    mine, theirs = side(core), side(1 - core)
    half = og.shape[1] // 2
    orders = (tuple(range(1, bits)), tuple(range(2, bits)) + (1,))
    halves = []
    for part, order in enumerate(orders):
        columns = og[:, part * half : (part + 1) * half]
        sent = exchange_bit((mm(theirs, columns, TN_DIMS) * norm).astype(jnp.bfloat16), 0)
        held = mm(mine, columns, TN_DIMS) * norm + sent.astype(jnp.float32)
        left = list(range(bits - 1, 0, -1))
        held = held.reshape((2,) * len(left) + (block, half))
        for bit in order:
            spot = left.index(bit)
            own = lax.rem(lax.div(place, 1 << bit), 2)
            away = lax.dynamic_index_in_dim(held, 1 - own, spot, keepdims=False)
            kept = lax.dynamic_index_in_dim(held, own, spot, keepdims=False)
            held = kept + exchange_bit(away.astype(jnp.bfloat16), bit).astype(jnp.float32)
            left.remove(bit)
        halves.append(held)
    return halves


def per_device(queries, key_rows, value_rows, out_grad, w_out, band_start, window_active):
    clip_count, tile_len, width = queries.shape
    seq_count = lax.axis_size("seq")
    seq_place = lax.axis_index("seq")
    steps = (1,) if seq_count == 2 else (1, -1)
    tile_index = jnp.mod(seq_place - band_start, seq_count)
    flags = (window_active[tile_index] == 1).astype(jnp.int32)
    times = (flags[:, 0] + flags[:, 2])[:, None] if seq_count == 2 else flags[:, 0::2]
    biases = jnp.where(times == 0, -jnp.inf, jnp.where(times == 2, 1.0, 0.0)).astype(jnp.float32)
    w_full = lax.all_gather(w_out, "dp", axis=0, tiled=True)
    spans = []
    first = 0
    for heads in CHUNKS:
        spans.append((first, heads))
        first += heads

    def cut(array, span):
        return array[:, span[0] * HS : (span[0] + span[1]) * HS]

    outs = []
    weight = None
    norm = 1.0 / math.sqrt(clip_count * lax.axis_size("dp") * seq_count * tile_len)
    for clip in range(clip_count):
        q, k, v, og = queries[clip], key_rows[clip], value_rows[clip], out_grad[clip]
        bias = biases[clip]
        others = []
        for span in spans:
            panel = jnp.stack((cut(k, span), cut(v, span)))
            others.append([passed_along(panel, "seq", step) for step in steps])
        att, lses = None, []
        for span, other in zip(spans, others):
            att, lse = forward(*span, bias, q, k, v, other, att)
            lses.append(lse)
        part = summed_rows(att, og, norm)
        weight = part if weight is None else [a + b for a, b in zip(weight, part)]
        dq, sums = None, ()
        pending = []
        for span, other, lse in zip(spans, others, lses):
            dq, own, away = backward(*span, bias, q, k, v, att, lse, og, w_full, other, dq)
            received = [passed_along(x, "seq", -step) for x, step in zip(away, steps)]
            pending.append((span, own, received))
        for span, own, received in pending:
            sums = add_parts(*span, tile_len, width, own, received, sums)
        outs.append((dq, *sums))
    if seq_count == 2:
        weight = [half.astype(jnp.bfloat16) for half in weight]
        weight = [
            half.astype(jnp.float32) + passed_along(half, "seq", 1).astype(jnp.float32)
            for half in weight
        ]
    else:
        weight = [lax.psum(half, "seq") for half in weight]
    grads = [jnp.stack(group) if clip_count > 1 else group[0][None] for group in zip(*outs)]
    return (*grads, jnp.concatenate(weight, axis=1))


def solution(mesh):
    rows = P("dp", "seq", None)
    return jax.shard_map(
        per_device,
        mesh=mesh,
        in_specs=(rows, rows, rows, rows, P("dp", None), P("dp"), P()),
        out_specs=(rows, rows, rows, P("dp", None)),
        check_vma=False,
    )
```

```python
import functools
import math

import jax
import jax.numpy as jnp
from jax import lax
from jax.experimental import pallas as pl
from jax.experimental.pallas import tpu as pltpu
from jax.sharding import PartitionSpec as P

HEADS = 12
HS = 128
CHUNKS = (4, 4, 4)
GRAD_CHUNKS = ((0, 0, 2), (0, 2, 2), (1, 0, 4), (2, 0, 4))
SCALE = HS ** (-0.5)
LOG2E = 1.4426950408889634
VMEM_LIMIT = 48 * 1024 * 1024

NT_DIMS = (((1,), (1,)), ((), ()))
TN_DIMS = (((0,), (0,)), ((), ()))
NN_DIMS = (((1,), (0,)), ((), ()))


def mm(lhs, rhs, dims):
    return lax.dot_general(lhs, rhs, dims, preferred_element_type=jnp.float32)


def passed_along(value, axis, steps):
    count = lax.axis_size(axis)
    pairs = [(source, (source + steps) % count) for source in range(count)]
    return lax.ppermute(value, axis, pairs)


def forward_kernel(other_count, bias_ref, q_ref, k_ref, v_ref, *refs):
    other_refs = refs[:other_count]
    att_ref, lse_ref = refs[-2:]
    query = q_ref[...]
    scores = [mm(k_ref[...], query, NT_DIMS) * (SCALE * LOG2E)]
    values = [v_ref[...]]
    for place, other_ref in enumerate(other_refs):
        scores.append(mm(other_ref[0], query, NT_DIMS) * (SCALE * LOG2E) + bias_ref[place])
        values.append(other_ref[1])
    row_max = functools.reduce(
        jnp.maximum, [jnp.max(block, axis=0, keepdims=True) for block in scores]
    )
    total = 0.0
    mixed = 0.0
    for block, value in zip(scores, values):
        weights = jnp.exp2(block - row_max)
        total = total + jnp.sum(weights, axis=0, keepdims=True)
        mixed = mixed + mm(value, weights.astype(jnp.bfloat16), TN_DIMS)
    att_ref[...] = (mixed / total).astype(att_ref.dtype)
    lse_ref[0] = jnp.broadcast_to(row_max + jnp.log2(total), lse_ref.shape[1:])


def backward_kernel(
    other_count, bias_ref, q_ref, k_ref, v_ref, att_ref, lse_ref, og_ref, w_ref, *refs
):
    other_refs = refs[:other_count]
    dq_ref, own_ref = refs[-2 - other_count : len(refs) - other_count]
    out_refs = refs[len(refs) - other_count :]
    query = q_ref[...]
    grad = mm(og_ref[...], w_ref[...], NT_DIMS).astype(jnp.bfloat16)
    turned = jnp.transpose(grad.astype(jnp.float32))
    delta = jnp.sum(turned * att_ref[...].astype(jnp.float32), axis=0, keepdims=True)
    log_total = lse_ref[0][0:1]
    query_part = 0.0
    for place in range(other_count + 1):
        if place == 0:
            key, value, shift = k_ref[...], v_ref[...], log_total
        else:
            key, value = other_refs[place - 1][0], other_refs[place - 1][1]
            shift = log_total - bias_ref[place - 1]
        prob = jnp.exp2(mm(key, query, NT_DIMS) * (SCALE * LOG2E) - shift)
        value_part = mm(prob.astype(jnp.bfloat16), grad, NN_DIMS)
        score_grad = (prob * (mm(value, grad, NT_DIMS) - delta)).astype(jnp.bfloat16)
        key_part = mm(score_grad, query, NN_DIMS) * SCALE
        query_part = query_part + mm(key, score_grad, TN_DIMS)
        target = own_ref if place == 0 else out_refs[place - 1]
        target[0] = key_part.astype(target.dtype)
        target[1] = value_part.astype(target.dtype)
    dq_ref[...] = jnp.transpose(query_part * SCALE).astype(dq_ref.dtype)


def add_kernel(other_count, own_ref, *refs):
    dk_ref, dv_ref = refs[-2:]
    keys, values = own_ref[0], own_ref[1]
    for ref in refs[:other_count]:
        keys = keys + ref[0].astype(jnp.float32)
        values = values + ref[1].astype(jnp.float32)
    dk_ref[...] = keys.astype(dk_ref.dtype)
    dv_ref[...] = values.astype(dv_ref.dtype)


def params():
    return pltpu.CompilerParams(vmem_limit_bytes=VMEM_LIMIT)


def cost(flops, moved, exps):
    return pl.CostEstimate(flops=int(flops), bytes_accessed=int(moved), transcendentals=int(exps))


def column_block(rows, first):
    return pl.BlockSpec((rows, HS), lambda i: (0, first + i))


def row_block(rows, first):
    return pl.BlockSpec((HS, rows), lambda i: (first + i, 0))


def pair_block(rows, skip=0):
    return pl.BlockSpec((2, rows, HS), lambda i: (0, 0, skip + i))


SMEM_BLOCK = pl.BlockSpec(memory_space=pltpu.SMEM)
HBM_BLOCK = pl.BlockSpec(memory_space=pl.ANY)


def forward(first, heads, bias, q, k, v, others, att):
    rows, width = q.shape
    count = len(others)
    head = column_block(rows, first)
    chained = [] if att is None else [att]
    return pl.pallas_call(
        functools.partial(forward_kernel, count),
        grid=(heads,),
        in_specs=[SMEM_BLOCK, head, head, head]
        + [pair_block(rows)] * count
        + [HBM_BLOCK] * len(chained),
        out_specs=[row_block(rows, first), pl.BlockSpec((1, 8, rows), lambda i: (i, 0, 0))],
        out_shape=[
            jax.ShapeDtypeStruct((width, rows), jnp.bfloat16),
            jax.ShapeDtypeStruct((heads, 8, rows), jnp.float32),
        ],
        input_output_aliases={4 + count: 0} if chained else {},
        compiler_params=params(),
        cost_estimate=cost(
            heads * (count + 1) * rows * rows * HS * 4,
            heads * rows * HS * 2 * (4 + 2 * count),
            heads * (count + 1) * rows * rows,
        ),
        name="attend",
    )(bias, q, k, v, *others, *chained)


def backward(first, skip, heads, bias, q, k, v, att, lse, og, w, others, dq):
    rows, width = q.shape
    count = len(others)
    head = column_block(rows, first)
    chained = [] if dq is None else [dq]
    results = pl.pallas_call(
        functools.partial(backward_kernel, count),
        grid=(heads,),
        in_specs=[SMEM_BLOCK, head, head, head, row_block(rows, first)]
        + [
            pl.BlockSpec((1, 8, rows), lambda i: (skip + i, 0, 0)),
            pl.BlockSpec(og.shape, lambda i: (0, 0)),
            pl.BlockSpec((HS, w.shape[1]), lambda i: (first + i, 0)),
        ]
        + [pair_block(rows, skip)] * count
        + [HBM_BLOCK] * len(chained),
        out_specs=[head] + [pair_block(rows)] * (count + 1),
        out_shape=[
            jax.ShapeDtypeStruct((rows, width), jnp.bfloat16),
            jax.ShapeDtypeStruct((2, rows, heads * HS), jnp.float32),
        ]
        + [jax.ShapeDtypeStruct((2, rows, heads * HS), jnp.bfloat16)] * count,
        input_output_aliases={8 + count: 0} if chained else {},
        compiler_params=params(),
        cost_estimate=cost(
            heads * ((count + 1) * rows * rows * HS * 10 + rows * HS * width * 2),
            heads * rows * HS * 2 * (8 + 8 * count),
            heads * (count + 1) * rows * rows,
        ),
        name="attend_grad",
    )(bias, q, k, v, att, lse, og, w, *others, *chained)
    return results[0], results[1], results[2:]


def add_parts(first, heads, rows, width, own, received, chained):
    count = len(received)
    head = column_block(rows, first)
    return pl.pallas_call(
        functools.partial(add_kernel, count),
        grid=(heads,),
        in_specs=[pair_block(rows)] * (count + 1) + [HBM_BLOCK] * len(chained),
        out_specs=[head, head],
        out_shape=[jax.ShapeDtypeStruct((rows, width), jnp.bfloat16)] * 2,
        input_output_aliases={1 + count: 0, 2 + count: 1} if chained else {},
        compiler_params=params(),
        cost_estimate=cost(0, heads * rows * HS * 2 * (6 + 2 * count), 0),
        name="add_parts",
    )(own, *received, *chained)


def exchange_bit(value, bit):
    count = lax.axis_size("dp")
    return lax.ppermute(value, "dp", [(source, source ^ (1 << bit)) for source in range(count)])


def after(value, earlier):
    return lax.optimization_barrier((value, earlier))[0]


def bit_of(place, bit):
    return lax.rem(lax.div(place, 1 << bit), 2)


def pick(array, which, axis):
    return lax.dynamic_index_in_dim(array, which, axis, keepdims=False)


class RowSums:
    def __init__(self, att, og, norm, hold):
        self.place = lax.axis_index("dp")
        bits = lax.axis_size("dp").bit_length() - 1
        width, tokens = att.shape
        block = width >> bits
        half = og.shape[1] // 2
        core = bit_of(self.place, 0)
        panels = att.reshape(width // (2 * block), 2, block, tokens)
        mine, theirs = (
            pick(panels, which, 1).reshape(width // 2, tokens) for which in (core, 1 - core)
        )
        columns = [og[:, :half], after(og[:, half:], hold)]
        shape = (2,) * (bits - 1) + (block, half)
        self.orders = [tuple(range(1, bits)), tuple(range(2, bits)) + (1,)]
        self.left = [list(range(bits - 1, 0, -1)) for _ in columns]
        self.sent = [
            (mm(theirs, part, NN_DIMS) * norm).astype(jnp.bfloat16) for part in columns
        ]
        self.got = [exchange_bit(part, 0).reshape(shape) for part in self.sent]
        self.kept = lambda: [
            (mm(mine, part, NN_DIMS) * norm).reshape(shape) for part in columns
        ]
        self.steps = bits - 1
        self.done = 0

    def totals(self, earlier):
        kept = self.kept()
        got = self.got if earlier is None else after(self.got, earlier)
        return [a + b.astype(jnp.float32) for a, b in zip(kept, got)]

    def step(self, earlier=None):
        held = self.totals(earlier)
        self.sent, self.got, kept = [], [], []
        for part, order, left in zip(held, self.orders, self.left):
            bit = order[self.done]
            spot = left.index(bit)
            own = bit_of(self.place, bit)
            self.sent.append(pick(part, 1 - own, spot).astype(jnp.bfloat16))
            self.got.append(exchange_bit(self.sent[-1], bit))
            kept.append(pick(part, own, spot))
            left.remove(bit)
        self.kept = lambda: kept
        self.done += 1

    def finish(self):
        while self.done < self.steps:
            self.step()
        return self.totals(None)


def per_device(queries, key_rows, value_rows, out_grad, w_out, band_start, window_active):
    clip_count, tile_len, width = queries.shape
    seq_count = lax.axis_size("seq")
    seq_place = lax.axis_index("seq")
    steps = (1,) if seq_count == 2 else (1, -1)
    tile_index = jnp.mod(seq_place - band_start, seq_count)
    flags = (window_active[tile_index] == 1).astype(jnp.int32)
    times = (flags[:, 0] + flags[:, 2])[:, None] if seq_count == 2 else flags[:, 0::2]
    biases = jnp.where(times == 0, -jnp.inf, jnp.where(times == 2, 1.0, 0.0)).astype(jnp.float32)
    w_full = lax.all_gather(w_out, "dp", axis=0, tiled=True)
    spans = []
    first = 0
    for heads in CHUNKS:
        spans.append((first, heads))
        first += heads

    def cut(array, span):
        return array[:, span[0] * HS : (span[0] + span[1]) * HS]

    outs = []
    weight = None
    norm = 1.0 / math.sqrt(clip_count * lax.axis_size("dp") * seq_count * tile_len)
    for clip in range(clip_count):
        q, k, v, og = queries[clip], key_rows[clip], value_rows[clip], out_grad[clip]
        bias = biases[clip]
        others, panel = [], None
        for span in spans:
            source = (k, v) if panel is None else after((k, v), panel)
            panel = jnp.stack([cut(array, span) for array in source])
            others.append([passed_along(panel, "seq", step) for step in steps])
        att, lses = None, []
        for span, other in zip(spans, others):
            att, lse = forward(*span, bias, q, k, v, other, att)
            lses.append(lse)
        dq, sums = None, ()
        pending = []
        sums_of_rows = None
        for turn, (panel, skip, heads) in enumerate(GRAD_CHUNKS):
            span = (spans[panel][0] + skip, heads)
            dq, own, away = backward(
                span[0], skip, heads, bias, q, k, v, att, lses[panel], og, w_full, others[panel], dq
            )
            received = [passed_along(x, "seq", -step) for x, step in zip(away, steps)]
            pending.append((span, own, received))
            if turn == 1:
                sums_of_rows = RowSums(after(att, away), og, norm, pending[0][2])
                bias = after(bias, sums_of_rows.sent)
            elif turn == 2:
                sums_of_rows.step((away, pending[1][2]))
                bias = after(bias, sums_of_rows.sent)
            elif turn == 3:
                sums_of_rows.step(away)
        part = sums_of_rows.finish()
        last_sent = part
        weight = part if weight is None else [a + b for a, b in zip(weight, part)]
        for span, own, received in pending:
            own = after(own, last_sent)
            sums = add_parts(*span, tile_len, width, own, received, sums)
        outs.append((dq, *sums))
    if seq_count == 2:
        weight = [half.astype(jnp.bfloat16) for half in weight]
        weight = [
            half.astype(jnp.float32) + passed_along(half, "seq", 1).astype(jnp.float32)
            for half in weight
        ]
    else:
        weight = [lax.psum(half, "seq") for half in weight]
    grads = [jnp.stack(group) if clip_count > 1 else group[0][None] for group in zip(*outs)]
    return (*grads, jnp.concatenate(weight, axis=1))


def solution(mesh):
    rows = P("dp", "seq", None)
    return jax.shard_map(
        per_device,
        mesh=mesh,
        in_specs=(rows, rows, rows, rows, P("dp", None), P("dp"), P()),
        out_specs=(rows, rows, rows, P("dp", None)),
        check_vma=False,
    )
```

```python
import functools
import math

import jax
import jax.numpy as jnp
from jax import lax
from jax.experimental import pallas as pl
from jax.experimental.pallas import tpu as pltpu
from jax.sharding import PartitionSpec as P

HEADS = 12
HS = 128
CHUNKS = (3, 3, 3, 3)
GRAD_CHUNKS = ((0, 0, 3), (1, 0, 3), (2, 0, 3), (3, 0, 3))
SCALE = HS ** (-0.5)
LOG2E = 1.4426950408889634
VMEM_LIMIT = 48 * 1024 * 1024

NT_DIMS = (((1,), (1,)), ((), ()))
TN_DIMS = (((0,), (0,)), ((), ()))
NN_DIMS = (((1,), (0,)), ((), ()))


def mm(lhs, rhs, dims):
    return lax.dot_general(lhs, rhs, dims, preferred_element_type=jnp.float32)


def passed_along(value, axis, steps):
    count = lax.axis_size(axis)
    pairs = [(source, (source + steps) % count) for source in range(count)]
    return lax.ppermute(value, axis, pairs)


def forward_kernel(other_count, bias_ref, q_ref, k_ref, v_ref, *refs):
    other_refs = refs[:other_count]
    att_ref, lse_ref = refs[-2:]
    query = q_ref[...]
    scores = [mm(k_ref[...], query, NT_DIMS) * (SCALE * LOG2E)]
    values = [v_ref[...]]
    for place, other_ref in enumerate(other_refs):
        scores.append(mm(other_ref[0], query, NT_DIMS) * (SCALE * LOG2E) + bias_ref[place])
        values.append(other_ref[1])
    row_max = functools.reduce(
        jnp.maximum, [jnp.max(block, axis=0, keepdims=True) for block in scores]
    )
    total = 0.0
    mixed = 0.0
    for block, value in zip(scores, values):
        weights = jnp.exp2(block - row_max)
        total = total + jnp.sum(weights, axis=0, keepdims=True)
        mixed = mixed + mm(value, weights.astype(jnp.bfloat16), TN_DIMS)
    att_ref[...] = (mixed / total).astype(att_ref.dtype)
    lse_ref[0] = jnp.broadcast_to(row_max + jnp.log2(total), lse_ref.shape[1:])


def backward_kernel(
    other_count, bias_ref, q_ref, k_ref, v_ref, att_ref, lse_ref, og_ref, w_ref, *refs
):
    other_refs = refs[:other_count]
    dq_ref, own_ref = refs[-2 - other_count : len(refs) - other_count]
    out_refs = refs[len(refs) - other_count :]
    query = q_ref[...]
    grad = mm(og_ref[...], w_ref[...], NT_DIMS).astype(jnp.bfloat16)
    turned = jnp.transpose(grad.astype(jnp.float32))
    delta = jnp.sum(turned * att_ref[...].astype(jnp.float32), axis=0, keepdims=True)
    log_total = lse_ref[0][0:1]
    query_part = 0.0
    for place in range(other_count + 1):
        if place == 0:
            key, value, shift = k_ref[...], v_ref[...], log_total
        else:
            key, value = other_refs[place - 1][0], other_refs[place - 1][1]
            shift = log_total - bias_ref[place - 1]
        prob = jnp.exp2(mm(key, query, NT_DIMS) * (SCALE * LOG2E) - shift)
        value_part = mm(prob.astype(jnp.bfloat16), grad, NN_DIMS)
        score_grad = (prob * (mm(value, grad, NT_DIMS) - delta)).astype(jnp.bfloat16)
        key_part = mm(score_grad, query, NN_DIMS) * SCALE
        query_part = query_part + mm(key, score_grad, TN_DIMS)
        target = own_ref if place == 0 else out_refs[place - 1]
        target[0] = key_part.astype(target.dtype)
        target[1] = value_part.astype(target.dtype)
    dq_ref[...] = jnp.transpose(query_part * SCALE).astype(dq_ref.dtype)


def add_kernel(other_count, own_ref, *refs):
    dk_ref, dv_ref = refs[-2:]
    keys, values = own_ref[0], own_ref[1]
    for ref in refs[:other_count]:
        keys = keys + ref[0].astype(jnp.float32)
        values = values + ref[1].astype(jnp.float32)
    dk_ref[...] = keys.astype(dk_ref.dtype)
    dv_ref[...] = values.astype(dv_ref.dtype)


def params():
    return pltpu.CompilerParams(vmem_limit_bytes=VMEM_LIMIT)


def cost(flops, moved, exps):
    return pl.CostEstimate(flops=int(flops), bytes_accessed=int(moved), transcendentals=int(exps))


def column_block(rows, first):
    return pl.BlockSpec((rows, HS), lambda i: (0, first + i))


def row_block(rows, first):
    return pl.BlockSpec((HS, rows), lambda i: (first + i, 0))


def pair_block(rows, skip=0):
    return pl.BlockSpec((2, rows, HS), lambda i: (0, 0, skip + i))


SMEM_BLOCK = pl.BlockSpec(memory_space=pltpu.SMEM)
HBM_BLOCK = pl.BlockSpec(memory_space=pl.ANY)


def forward(first, heads, bias, q, k, v, others, att):
    rows, width = q.shape
    count = len(others)
    head = column_block(rows, first)
    chained = [] if att is None else [att]
    return pl.pallas_call(
        functools.partial(forward_kernel, count),
        grid=(heads,),
        in_specs=[SMEM_BLOCK, head, head, head]
        + [pair_block(rows)] * count
        + [HBM_BLOCK] * len(chained),
        out_specs=[row_block(rows, first), pl.BlockSpec((1, 8, rows), lambda i: (i, 0, 0))],
        out_shape=[
            jax.ShapeDtypeStruct((width, rows), jnp.bfloat16),
            jax.ShapeDtypeStruct((heads, 8, rows), jnp.float32),
        ],
        input_output_aliases={4 + count: 0} if chained else {},
        compiler_params=params(),
        cost_estimate=cost(
            heads * (count + 1) * rows * rows * HS * 4,
            heads * rows * HS * 2 * (4 + 2 * count),
            heads * (count + 1) * rows * rows,
        ),
        name="attend",
    )(bias, q, k, v, *others, *chained)


def backward(first, skip, heads, bias, q, k, v, att, lse, og, w, others, dq):
    rows, width = q.shape
    count = len(others)
    head = column_block(rows, first)
    chained = [] if dq is None else [dq]
    results = pl.pallas_call(
        functools.partial(backward_kernel, count),
        grid=(heads,),
        in_specs=[SMEM_BLOCK, head, head, head, row_block(rows, first)]
        + [
            pl.BlockSpec((1, 8, rows), lambda i: (skip + i, 0, 0)),
            pl.BlockSpec(og.shape, lambda i: (0, 0)),
            pl.BlockSpec((HS, w.shape[1]), lambda i: (first + i, 0)),
        ]
        + [pair_block(rows, skip)] * count
        + [HBM_BLOCK] * len(chained),
        out_specs=[head] + [pair_block(rows)] * (count + 1),
        out_shape=[
            jax.ShapeDtypeStruct((rows, width), jnp.bfloat16),
            jax.ShapeDtypeStruct((2, rows, heads * HS), jnp.float32),
        ]
        + [jax.ShapeDtypeStruct((2, rows, heads * HS), jnp.bfloat16)] * count,
        input_output_aliases={8 + count: 0} if chained else {},
        compiler_params=params(),
        cost_estimate=cost(1000, 1000, 0),
        name="attend_grad",
    )(bias, q, k, v, att, lse, og, w, *others, *chained)
    return results[0], results[1], results[2:]


def add_parts(first, heads, rows, width, own, received, chained):
    count = len(received)
    head = column_block(rows, first)
    return pl.pallas_call(
        functools.partial(add_kernel, count),
        grid=(heads,),
        in_specs=[pair_block(rows)] * (count + 1) + [HBM_BLOCK] * len(chained),
        out_specs=[head, head],
        out_shape=[jax.ShapeDtypeStruct((rows, width), jnp.bfloat16)] * 2,
        input_output_aliases={1 + count: 0, 2 + count: 1} if chained else {},
        compiler_params=params(),
        cost_estimate=cost(0, heads * rows * HS * 2 * (6 + 2 * count), 0),
        name="add_parts",
    )(own, *received, *chained)


def exchange_bit(value, bit):
    count = lax.axis_size("dp")
    return lax.ppermute(value, "dp", [(source, source ^ (1 << bit)) for source in range(count)])


def after(value, earlier):
    return lax.optimization_barrier((value, earlier))[0]


def bit_of(place, bit):
    return lax.rem(lax.div(place, 1 << bit), 2)


def pick(array, which, axis):
    return lax.dynamic_index_in_dim(array, which, axis, keepdims=False)


class RowSums:
    def __init__(self, att, og, norm):
        self.place = lax.axis_index("dp")
        bits = lax.axis_size("dp").bit_length() - 1
        width, tokens = att.shape
        block = width >> bits
        half = og.shape[1] // 2
        core = bit_of(self.place, 0)
        panels = att.reshape(width // (2 * block), 2, block, tokens)
        mine, theirs = (
            pick(panels, which, 1).reshape(width // 2, tokens) for which in (core, 1 - core)
        )
        columns = [og[:, :half], og[:, half:]]
        shape = (2,) * (bits - 1) + (block, half)
        self.orders = [tuple(range(1, bits)), tuple(range(2, bits)) + (1,)]
        self.left = [list(range(bits - 1, 0, -1)) for _ in columns]
        self.sent = [
            (mm(theirs, part, NN_DIMS) * norm).astype(jnp.bfloat16) for part in columns
        ]
        self.got = [exchange_bit(part, 0).reshape(shape) for part in self.sent]
        self.kept = lambda: [
            (mm(mine, part, NN_DIMS) * norm).reshape(shape) for part in columns
        ]
        self.steps = bits - 1
        self.done = 0

    def totals(self, earlier):
        kept = self.kept()
        got = self.got if earlier is None else after(self.got, earlier)
        return [a + b.astype(jnp.float32) for a, b in zip(kept, got)]

    def step(self, earlier=None):
        held = self.totals(earlier)
        self.sent, self.got, kept = [], [], []
        for part, order, left in zip(held, self.orders, self.left):
            bit = order[self.done]
            spot = left.index(bit)
            own = bit_of(self.place, bit)
            self.sent.append(pick(part, 1 - own, spot).astype(jnp.bfloat16))
            self.got.append(exchange_bit(self.sent[-1], bit))
            kept.append(pick(part, own, spot))
            left.remove(bit)
        self.kept = lambda: kept
        self.done += 1

    def finish(self):
        while self.done < self.steps:
            self.step()
        return self.totals(None)


def per_device(queries, key_rows, value_rows, out_grad, w_out, band_start, window_active):
    clip_count, tile_len, width = queries.shape
    seq_count = lax.axis_size("seq")
    seq_place = lax.axis_index("seq")
    steps = (1,) if seq_count == 2 else (1, -1)
    tile_index = jnp.mod(seq_place - band_start, seq_count)
    flags = (window_active[tile_index] == 1).astype(jnp.int32)
    times = (flags[:, 0] + flags[:, 2])[:, None] if seq_count == 2 else flags[:, 0::2]
    biases = jnp.where(times == 0, -jnp.inf, jnp.where(times == 2, 1.0, 0.0)).astype(jnp.float32)
    w_full = lax.all_gather(w_out, "dp", axis=0, tiled=True)
    spans = []
    first = 0
    for heads in CHUNKS:
        spans.append((first, heads))
        first += heads

    def cut(array, span):
        return array[:, span[0] * HS : (span[0] + span[1]) * HS]

    outs = []
    weight = None
    norm = 1.0 / math.sqrt(clip_count * lax.axis_size("dp") * seq_count * tile_len)
    for clip in range(clip_count):
        q, k, v, og = queries[clip], key_rows[clip], value_rows[clip], out_grad[clip]
        bias = biases[clip]
        others, panel = [], None
        for span in spans:
            source = (k, v) if panel is None else after((k, v), panel)
            panel = jnp.stack([cut(array, span) for array in source])
            others.append([passed_along(panel, "seq", step) for step in steps])
        att, lses = None, []
        for span, other in zip(spans, others):
            att, lse = forward(*span, bias, q, k, v, other, att)
            lses.append(lse)
        dq, sums = None, ()
        pending = []
        sums_of_rows = None
        for turn, (panel, skip, heads) in enumerate(GRAD_CHUNKS):
            span = (spans[panel][0] + skip, heads)
            dq, own, away = backward(
                span[0], skip, heads, bias, q, k, v, att, lses[panel], og, w_full, others[panel], dq
            )
            received = [passed_along(x, "seq", -step) for x, step in zip(away, steps)]
            pending.append((span, own, received))
            if turn == 0:
                sums_of_rows = RowSums(after(att, away), og, norm)
            else:
                sums_of_rows.step((away, pending[turn - 1][2]))
            bias = after(bias, sums_of_rows.sent)
        part = sums_of_rows.finish()
        last_sent = part
        weight = part if weight is None else [a + b for a, b in zip(weight, part)]
        for span, own, received in pending:
            own = after(own, last_sent)
            sums = add_parts(*span, tile_len, width, own, received, sums)
        outs.append((dq, *sums))
    if seq_count == 2:
        weight = [half.astype(jnp.bfloat16) for half in weight]
        weight = [
            half.astype(jnp.float32) + passed_along(half, "seq", 1).astype(jnp.float32)
            for half in weight
        ]
    else:
        weight = [lax.psum(half, "seq") for half in weight]
    grads = [jnp.stack(group) if clip_count > 1 else group[0][None] for group in zip(*outs)]
    return (*grads, jnp.concatenate(weight, axis=1))


def solution(mesh):
    rows = P("dp", "seq", None)
    return jax.shard_map(
        per_device,
        mesh=mesh,
        in_specs=(rows, rows, rows, rows, P("dp", None), P("dp"), P()),
        out_specs=(rows, rows, rows, P("dp", None)),
        check_vma=False,
    )
```

```python
import functools
import math

import jax
import jax.numpy as jnp
from jax import lax
from jax.experimental import pallas as pl
from jax.experimental.pallas import tpu as pltpu
from jax.sharding import PartitionSpec as P

HEADS = 12
HS = 128
CHUNKS = (3, 4, 3, 2)
GRAD_CHUNKS = ((0, 0, 3), (1, 0, 4), (2, 0, 3), (3, 0, 2))
SCALE = HS ** (-0.5)
LOG2E = 1.4426950408889634
VMEM_LIMIT = 48 * 1024 * 1024

NT_DIMS = (((1,), (1,)), ((), ()))
TN_DIMS = (((0,), (0,)), ((), ()))
NN_DIMS = (((1,), (0,)), ((), ()))


def mm(lhs, rhs, dims):
    return lax.dot_general(lhs, rhs, dims, preferred_element_type=jnp.float32)


def passed_along(value, axis, steps):
    count = lax.axis_size(axis)
    pairs = [(source, (source + steps) % count) for source in range(count)]
    return lax.ppermute(value, axis, pairs)


def forward_kernel(other_count, bias_ref, q_ref, k_ref, v_ref, *refs):
    other_refs = refs[:other_count]
    att_ref, lse_ref = refs[-2:]
    query = q_ref[...]
    scores = [mm(k_ref[...], query, NT_DIMS) * (SCALE * LOG2E)]
    values = [v_ref[...]]
    for place, other_ref in enumerate(other_refs):
        scores.append(mm(other_ref[0], query, NT_DIMS) * (SCALE * LOG2E) + bias_ref[place])
        values.append(other_ref[1])
    row_max = functools.reduce(
        jnp.maximum, [jnp.max(block, axis=0, keepdims=True) for block in scores]
    )
    total = 0.0
    mixed = 0.0
    for block, value in zip(scores, values):
        weights = jnp.exp2(block - row_max)
        total = total + jnp.sum(weights, axis=0, keepdims=True)
        mixed = mixed + mm(value, weights.astype(jnp.bfloat16), TN_DIMS)
    att_ref[...] = (mixed / total).astype(att_ref.dtype)
    lse_ref[0] = jnp.broadcast_to(row_max + jnp.log2(total), lse_ref.shape[1:])


def backward_kernel(
    other_count, bias_ref, q_ref, k_ref, v_ref, att_ref, lse_ref, og_ref, w_ref, *refs
):
    other_refs = refs[:other_count]
    dq_ref, own_ref = refs[-2 - other_count : len(refs) - other_count]
    out_refs = refs[len(refs) - other_count :]
    query = q_ref[...]
    grad = mm(og_ref[...], w_ref[...], NT_DIMS).astype(jnp.bfloat16)
    turned = jnp.transpose(grad.astype(jnp.float32))
    delta = jnp.sum(turned * att_ref[...].astype(jnp.float32), axis=0, keepdims=True)
    log_total = lse_ref[0][0:1]
    query_part = 0.0
    for place in range(other_count + 1):
        if place == 0:
            key, value, shift = k_ref[...], v_ref[...], log_total
        else:
            key, value = other_refs[place - 1][0], other_refs[place - 1][1]
            shift = log_total - bias_ref[place - 1]
        prob = jnp.exp2(mm(key, query, NT_DIMS) * (SCALE * LOG2E) - shift)
        value_part = mm(prob.astype(jnp.bfloat16), grad, NN_DIMS)
        score_grad = (prob * (mm(value, grad, NT_DIMS) - delta)).astype(jnp.bfloat16)
        key_part = mm(score_grad, query, NN_DIMS) * SCALE
        query_part = query_part + mm(key, score_grad, TN_DIMS)
        target = own_ref if place == 0 else out_refs[place - 1]
        target[0] = key_part.astype(target.dtype)
        target[1] = value_part.astype(target.dtype)
    dq_ref[...] = jnp.transpose(query_part * SCALE).astype(dq_ref.dtype)


def add_kernel(other_count, own_ref, *refs):
    dk_ref, dv_ref = refs[-2:]
    keys, values = own_ref[0], own_ref[1]
    for ref in refs[:other_count]:
        keys = keys + ref[0].astype(jnp.float32)
        values = values + ref[1].astype(jnp.float32)
    dk_ref[...] = keys.astype(dk_ref.dtype)
    dv_ref[...] = values.astype(dv_ref.dtype)


def params():
    return pltpu.CompilerParams(vmem_limit_bytes=VMEM_LIMIT)


def cost(flops, moved, exps):
    return pl.CostEstimate(flops=int(flops), bytes_accessed=int(moved), transcendentals=int(exps))


def column_block(rows, first):
    return pl.BlockSpec((rows, HS), lambda i: (0, first + i))


def row_block(rows, first):
    return pl.BlockSpec((HS, rows), lambda i: (first + i, 0))


def pair_block(rows, skip=0):
    return pl.BlockSpec((2, rows, HS), lambda i: (0, 0, skip + i))


SMEM_BLOCK = pl.BlockSpec(memory_space=pltpu.SMEM)
HBM_BLOCK = pl.BlockSpec(memory_space=pl.ANY)


def forward(first, heads, bias, q, k, v, others, att):
    rows, width = q.shape
    count = len(others)
    head = column_block(rows, first)
    chained = [] if att is None else [att]
    return pl.pallas_call(
        functools.partial(forward_kernel, count),
        grid=(heads,),
        in_specs=[SMEM_BLOCK, head, head, head]
        + [pair_block(rows)] * count
        + [HBM_BLOCK] * len(chained),
        out_specs=[row_block(rows, first), pl.BlockSpec((1, 8, rows), lambda i: (i, 0, 0))],
        out_shape=[
            jax.ShapeDtypeStruct((width, rows), jnp.bfloat16),
            jax.ShapeDtypeStruct((heads, 8, rows), jnp.float32),
        ],
        input_output_aliases={4 + count: 0} if chained else {},
        compiler_params=params(),
        cost_estimate=cost(
            heads * (count + 1) * rows * rows * HS * 4,
            heads * rows * HS * 2 * (4 + 2 * count),
            heads * (count + 1) * rows * rows,
        ),
        name="attend",
    )(bias, q, k, v, *others, *chained)


def backward(first, skip, heads, bias, q, k, v, att, lse, og, w, others, dq):
    rows, width = q.shape
    count = len(others)
    head = column_block(rows, first)
    chained = [] if dq is None else [dq]
    results = pl.pallas_call(
        functools.partial(backward_kernel, count),
        grid=(heads,),
        in_specs=[SMEM_BLOCK, head, head, head, row_block(rows, first)]
        + [
            pl.BlockSpec((1, 8, rows), lambda i: (skip + i, 0, 0)),
            pl.BlockSpec(og.shape, lambda i: (0, 0)),
            pl.BlockSpec((HS, w.shape[1]), lambda i: (first + i, 0)),
        ]
        + [pair_block(rows, skip)] * count
        + [HBM_BLOCK] * len(chained),
        out_specs=[head] + [pair_block(rows)] * (count + 1),
        out_shape=[
            jax.ShapeDtypeStruct((rows, width), jnp.bfloat16),
            jax.ShapeDtypeStruct((2, rows, heads * HS), jnp.float32),
        ]
        + [jax.ShapeDtypeStruct((2, rows, heads * HS), jnp.bfloat16)] * count,
        input_output_aliases={8 + count: 0} if chained else {},
        compiler_params=params(),
        cost_estimate=cost(1000, 1000, 0),
        name="attend_grad",
    )(bias, q, k, v, att, lse, og, w, *others, *chained)
    return results[0], results[1], results[2:]


def add_parts(first, heads, rows, width, own, received, chained):
    count = len(received)
    head = column_block(rows, first)
    return pl.pallas_call(
        functools.partial(add_kernel, count),
        grid=(heads,),
        in_specs=[pair_block(rows)] * (count + 1) + [HBM_BLOCK] * len(chained),
        out_specs=[head, head],
        out_shape=[jax.ShapeDtypeStruct((rows, width), jnp.bfloat16)] * 2,
        input_output_aliases={1 + count: 0, 2 + count: 1} if chained else {},
        compiler_params=params(),
        cost_estimate=cost(0, heads * rows * HS * 2 * (6 + 2 * count), 0),
        name="add_parts",
    )(own, *received, *chained)


def exchange_bit(value, bit):
    count = lax.axis_size("dp")
    return lax.ppermute(value, "dp", [(source, source ^ (1 << bit)) for source in range(count)])


def after(value, earlier):
    return lax.optimization_barrier((value, earlier))[0]


def bit_of(place, bit):
    return lax.rem(lax.div(place, 1 << bit), 2)


def pick(array, which, axis):
    return lax.dynamic_index_in_dim(array, which, axis, keepdims=False)


class RowSums:
    def __init__(self, att, og, norm):
        self.place = lax.axis_index("dp")
        bits = lax.axis_size("dp").bit_length() - 1
        width, tokens = att.shape
        block = width >> bits
        half = og.shape[1] // 2
        core = bit_of(self.place, 0)
        panels = att.reshape(width // (2 * block), 2, block, tokens)
        mine, theirs = (
            pick(panels, which, 1).reshape(width // 2, tokens) for which in (core, 1 - core)
        )
        columns = [og[:, :half], og[:, half:]]
        shape = (2,) * (bits - 1) + (block, half)
        self.orders = [tuple(range(1, bits)), tuple(range(2, bits)) + (1,)]
        self.left = [list(range(bits - 1, 0, -1)) for _ in columns]
        self.sent = [
            (mm(theirs, part, NN_DIMS) * norm).astype(jnp.bfloat16) for part in columns
        ]
        self.got = [exchange_bit(part, 0).reshape(shape) for part in self.sent]
        self.kept = lambda: [
            (mm(mine, part, NN_DIMS) * norm).reshape(shape) for part in columns
        ]
        self.steps = bits - 1
        self.done = 0

    def totals(self, earlier):
        kept = self.kept()
        got = self.got if earlier is None else after(self.got, earlier)
        return [a + b.astype(jnp.float32) for a, b in zip(kept, got)]

    def step(self, earlier=None):
        held = self.totals(earlier)
        self.sent, self.got, kept = [], [], []
        for part, order, left in zip(held, self.orders, self.left):
            bit = order[self.done]
            spot = left.index(bit)
            own = bit_of(self.place, bit)
            self.sent.append(pick(part, 1 - own, spot).astype(jnp.bfloat16))
            self.got.append(exchange_bit(self.sent[-1], bit))
            kept.append(pick(part, own, spot))
            left.remove(bit)
        self.kept = lambda: kept
        self.done += 1

    def finish(self):
        while self.done < self.steps:
            self.step()
        return self.totals(None)


def per_device(queries, key_rows, value_rows, out_grad, w_out, band_start, window_active):
    clip_count, tile_len, width = queries.shape
    seq_count = lax.axis_size("seq")
    seq_place = lax.axis_index("seq")
    steps = (1,) if seq_count == 2 else (1, -1)
    tile_index = jnp.mod(seq_place - band_start, seq_count)
    flags = (window_active[tile_index] == 1).astype(jnp.int32)
    times = (flags[:, 0] + flags[:, 2])[:, None] if seq_count == 2 else flags[:, 0::2]
    biases = jnp.where(times == 0, -jnp.inf, jnp.where(times == 2, 1.0, 0.0)).astype(jnp.float32)
    w_full = lax.all_gather(w_out, "dp", axis=0, tiled=True)
    spans = []
    first = 0
    for heads in CHUNKS:
        spans.append((first, heads))
        first += heads

    def cut(array, span):
        return array[:, span[0] * HS : (span[0] + span[1]) * HS]

    outs = []
    weight = None
    norm = 1.0 / math.sqrt(clip_count * lax.axis_size("dp") * seq_count * tile_len)
    for clip in range(clip_count):
        q, k, v, og = queries[clip], key_rows[clip], value_rows[clip], out_grad[clip]
        bias = biases[clip]
        others, panel = [], None
        for span in spans:
            source = (k, v) if panel is None else after((k, v), panel)
            panel = jnp.stack([cut(array, span) for array in source])
            others.append([passed_along(panel, "seq", step) for step in steps])
        att, lses = None, []
        for span, other in zip(spans, others):
            att, lse = forward(*span, bias, q, k, v, other, att)
            lses.append(lse)
        dq, sums = None, ()
        pending = []
        sums_of_rows = None
        for turn, (panel, skip, heads) in enumerate(GRAD_CHUNKS):
            span = (spans[panel][0] + skip, heads)
            dq, own, away = backward(
                span[0], skip, heads, bias, q, k, v, att, lses[panel], og, w_full, others[panel], dq
            )
            received = [passed_along(x, "seq", -step) for x, step in zip(away, steps)]
            pending.append((span, own, received))
            if turn == 0:
                sums_of_rows = RowSums(after(att, away), og, norm)
            else:
                sums_of_rows.step((away, pending[turn - 1][2]))
            bias = after(bias, sums_of_rows.sent)
        early_sent = sums_of_rows.sent
        part = sums_of_rows.finish()
        last_sent = part
        weight = part if weight is None else [a + b for a, b in zip(weight, part)]
        for turn, (span, own, received) in enumerate(pending):
            own = after(own, early_sent if turn < 2 else last_sent)
            sums = add_parts(*span, tile_len, width, own, received, sums)
        outs.append((dq, *sums))
    if seq_count == 2:
        weight = [half.astype(jnp.bfloat16) for half in weight]
        weight = [
            half.astype(jnp.float32) + passed_along(half, "seq", 1).astype(jnp.float32)
            for half in weight
        ]
    else:
        weight = [lax.psum(half, "seq") for half in weight]
    grads = [jnp.stack(group) if clip_count > 1 else group[0][None] for group in zip(*outs)]
    return (*grads, jnp.concatenate(weight, axis=1))


def solution(mesh):
    rows = P("dp", "seq", None)
    return jax.shard_map(
        per_device,
        mesh=mesh,
        in_specs=(rows, rows, rows, rows, P("dp", None), P("dp"), P()),
        out_specs=(rows, rows, rows, P("dp", None)),
        check_vma=False,
    )
```
